32 devices in a mesh: energy: 8 (over y, x, core), slab: 4 (over z).
Axes of the slice: x: 2, y: 2, z: 4, core: 2. Of those that a mesh axis runs over, the one named last changes fastest.
Arguments:
- green_diag: float32 [4, 256, 2, 128, 128], P('slab', 'energy'), may hold values from -0.375 to 0.375
- green_lower: float32 [4, 256, 2, 128, 128], P('slab', 'energy'), may hold values from -0.375 to 0.375
- green_upper: float32 [4, 256, 2, 128, 128], P('slab', 'energy'), may hold values from -0.375 to 0.375
- sigma_lesser: float32 [4, 256, 2, 128, 128], P('slab', 'energy'), may hold values from -6 to 6
- screened: float32 [4, 256, 2, 128, 128], P('slab', None, None, 'energy'), may hold values from -6 to 6
- pattern: int32 [4, 128], P('slab'), may hold values 0 or 1
Outputs:
- green_lesser: float32 [4, 256, 2, 128, 128], P('slab', 'energy')
The draws below stay inside these ranges and needn't reach their ends.
All inputs are finite; a program needn't handle non-finite values. No bound on the sum of `pattern` on one device may be relied on, other than what follows from the above.
Results may differ from the reference program's by a relative error of at most 0.0001.
Values sent between devices are 32-bit elements; how exact they have to be, the bound alone decides.
No kernel may reach another device: no remote copies, remote signals or barrier semaphores. Data moves between devices by JAX's collectives and lax.ppermute only.
A program may use at most 128 MiB of HBM per device.

```python
import jax
import jax.numpy as jnp
from jax import lax

B = 128
E = 256
NBLK = 4


def with_ends(drawn, own_key, low, largest):
    dims = drawn.shape
    place = [jax.random.randint(jax.random.fold_in(own_key, axis), (), 0, dims[axis]) for axis in range(len(dims))]
    drawn = drawn.at[tuple(place)].set(low)
    longest = dims.index(max(dims))
    place[longest] = (place[longest] + 1) % dims[longest]
    return drawn.at[tuple(place)].set(largest)


def level_of(rng, shape, shards, least, largest):
    factor_of = 1.0
    for axis_at, blocks in shards:
        draws = jax.random.uniform(jax.random.fold_in(jax.random.fold_in(rng, 6), axis_at), (blocks,), jnp.float32, least / len(shards), largest / len(shards))
        factor_of = factor_of * jnp.repeat(jnp.exp(draws), shape[axis_at] // blocks).reshape((-1,) + (1,) * (len(shape) - 1 - axis_at))
    return factor_of


def normal_values(stream_key, shape, spread, reach, shards=(), kind=jnp.bfloat16):
    gain = level_of(stream_key, shape, shards, -0.22, 0.18) if shards else 1.0
    values = jax.random.normal(stream_key, shape, jnp.float32) * spread * gain
    return jnp.minimum(jnp.maximum(values, -reach), reach).astype(kind)


def setup_inputs(seed: int = 0) -> dict:
    key_list = jax.random.split(jax.random.key(seed), 7)
    return {
        "green_diag": normal_values(key_list[0], (NBLK, E, 2, B, B), (2 * B) ** -0.5, 0.375, ((0, 4), (1, 8)), jnp.float32),
        "green_lower": normal_values(key_list[1], (NBLK, E, 2, B, B), (2 * B) ** -0.5, 0.375, ((0, 4), (1, 8)), jnp.float32),
        "green_upper": normal_values(key_list[2], (NBLK, E, 2, B, B), (2 * B) ** -0.5, 0.375, ((0, 4), (1, 8)), jnp.float32),
        "sigma_lesser": normal_values(key_list[3], (NBLK, E, 2, B, B), 1.0, 6.0, ((0, 4), (1, 8)), jnp.float32),
        "screened": normal_values(key_list[4], (NBLK, E, 2, B, B), 1.0, 6.0, ((0, 4), (3, 8)), jnp.float32),
        "pattern": with_ends((jax.random.randint(key_list[5], (NBLK, B), 0, 2) < 1).astype(jnp.int32), jax.random.fold_in(key_list[5], 1), 0, 1),
    }


def matmul_plain(first_op, second_op):
    return jnp.einsum("...ab,...bc->...ac", first_op, second_op, precision=lax.Precision.HIGHEST)


def matmul_adjoint(first_op, second_op):
    return jnp.einsum("...ab,...cb->...ac", first_op, second_op, precision=lax.Precision.HIGHEST)


def sandwich(outer_factor, middle_factor):
    outer_real = outer_factor[..., 0, :, :]
    outer_imag = outer_factor[..., 1, :, :]
    middle_real = middle_factor[..., 0, :, :]
    middle_imag = middle_factor[..., 1, :, :]
    prod_real = matmul_plain(outer_real, middle_real) - matmul_plain(outer_imag, middle_imag)
    prod_imag = matmul_plain(outer_real, middle_imag) + matmul_plain(outer_imag, middle_real)
    final_real = matmul_adjoint(prod_real, outer_real) + matmul_adjoint(prod_imag, outer_imag)
    final_imag = matmul_adjoint(prod_imag, outer_real) - matmul_adjoint(prod_real, outer_imag)
    return jnp.stack([final_real, final_imag], axis=-3)


def lesser_product(green_diag, green_lower, green_upper, sigma_blocks):
    block_count = sigma_blocks.shape[0]
    results = []
    for index in range(block_count):
        total = sandwich(green_diag[index], sigma_blocks[index])
        if index > 0:
            total = total + sandwich(green_lower[index], sigma_blocks[index - 1])
        if index + 1 < block_count:
            total = total + sandwich(green_upper[index], sigma_blocks[index + 1])
        results.append(total)
    return jnp.stack(results, axis=0)


def reference(green_diag, green_lower, green_upper, sigma_lesser, screened, pattern):
    first_pass = lesser_product(green_diag, green_lower, green_upper, sigma_lesser)
    updated = []
    for index in range(first_pass.shape[0]):
        values = lax.complex(first_pass[index, :, 0], first_pass[index, :, 1])
        spectrum = jnp.fft.fft(values, axis=0)
        weights = lax.complex(screened[index, :, 0], screened[index, :, 1])
        convolved = jnp.fft.ifft(spectrum * weights, axis=0)
        scatter_part = jnp.stack([-jnp.imag(convolved), jnp.real(convolved)], axis=1)
        mask_float = pattern[index].astype(jnp.float32)
        kept = mask_float[:, None] * mask_float[None, :]
        updated.append(sigma_lesser[index] + kept[None, None] * scatter_part)
    sigma_new = jnp.stack(updated, axis=0)
    return lesser_product(green_diag, green_lower, green_upper, sigma_new)
```

```python
import functools

import jax
import jax.numpy as jnp
import numpy as np
from jax import lax
from jax.experimental import pallas as pl
from jax.experimental.pallas import tpu as pltpu
from jax.sharding import PartitionSpec as P

F32 = jnp.float32
BF16 = jnp.bfloat16
VMEM_LIMIT = 56 * 1024 * 1024


def params():
    return pltpu.CompilerParams(vmem_limit_bytes=VMEM_LIMIT)


def split(value):
    high = value.astype(BF16)
    return high, (value - high.astype(F32)).astype(BF16)


def dot(first, second, transposed=False):
    dims = (((1,), (1,)), ((), ())) if transposed else (((1,), (0,)), ((), ()))
    return lax.dot_general(first, second, dims, preferred_element_type=F32)


def dot3(first, second, transposed=False):
    rows = first[0].shape[0]
    both = dot(jnp.concatenate(first, axis=0), second[0], transposed)
    return both[:rows] + (both[rows:] + dot(first[0], second[1], transposed))


def complex_rows(pair):
    width = pair.shape[1] // 2
    turned = jnp.concatenate([-pair[:, width:], pair[:, :width]], axis=1)
    return jnp.concatenate([pair, turned], axis=0)


def load_matrix(ref, index):
    lead = (0,) * (len(ref.shape) - 4)
    return jnp.concatenate([ref[lead + (index, 0)], ref[lead + (index, 1)]], axis=1)


def load_rows(ref, index):
    groups, _, double, _ = ref.shape
    rows = double // 2
    parts = [jnp.concatenate([ref[r, index, p * rows : (p + 1) * rows, :] for r in range(groups)], axis=0) for p in (0, 1)]
    return jnp.concatenate(parts, axis=1)


def store_matrix(ref, index, value):
    width = value.shape[1] // 2
    lead = (0,) * (len(ref.shape) - 4)
    ref[lead + (index, 0)] = value[:, :width]
    ref[lead + (index, 1)] = value[:, width:]


def store_rows(ref, index, value):
    groups, _, double, width = ref.shape
    rows = double // 2
    for r in range(groups):
        for p in (0, 1):
            ref[r, index, p * rows : (p + 1) * rows, :] = value[r * rows : (r + 1) * rows, p * width : (p + 1) * width]


def sandwich(green, middle):
    green_pair = split(green)
    middle_pair = split(middle)
    first = dot3(green_pair, [complex_rows(part) for part in middle_pair])
    return dot3(split(first), [complex_rows(part) for part in green_pair], transposed=True)


def terms_kernel(count, load_base, load_middle, store, step, *refs):
    base = refs[0] if load_base is not None else None
    rest = refs[1:] if load_base is not None else refs
    greens, middles, out = rest[:count], rest[count : 2 * count], rest[-1]
    for index in range(step):
        total = load_base(base, index) if load_base is not None else None
        for green, middle in zip(greens, middles):
            term = sandwich(load_matrix(green, index), load_middle(middle, index))
            total = term if total is None else total + term
        store(out, index, total)


def matrix_spec(step, offset, width, lead):
    shape = (1,) * lead + (step, 2, width, width)
    return pl.BlockSpec(shape, lambda i: (0,) * lead + (i + offset, 0, 0, 0))


def rows_spec(step, groups, rows, width):
    return pl.BlockSpec((groups, step, 2 * rows, width), lambda i: (0, i, 0, 0))


def cost(energies, count, width):
    return pl.CostEstimate(
        flops=energies * count * 12 * 4 * width**3,
        bytes_accessed=energies * (2 * count + 2) * 8 * width * width,
        transcendentals=0,
    )


def own_terms(green, sigma, step):
    _, energies, _, width, _ = green.shape
    return pl.pallas_call(
        functools.partial(terms_kernel, 1, None, load_matrix, store_matrix, step),
        grid=(energies // step,),
        in_specs=[matrix_spec(step, 0, width, 1)] * 2,
        out_specs=matrix_spec(step, 0, width, 0),
        out_shape=jax.ShapeDtypeStruct((energies, 2, width, width), F32),
        compiler_params=params(),
        cost_estimate=cost(energies, 1, width),
        name="own_terms",
    )(green, sigma)


def side_terms(own, lower, upper, before, after, begin, size, groups, step):
    energies, _, width, _ = own.shape
    rows = width // groups
    at = begin // step
    return pl.pallas_call(
        functools.partial(terms_kernel, 2, load_matrix, load_matrix, store_rows, step),
        grid=(size // step,),
        in_specs=[matrix_spec(step, at, width, 0)] + [matrix_spec(step, at, width, 1)] * 2 + [matrix_spec(step, 0, width, 1)] * 2,
        out_specs=rows_spec(step, groups, rows, width),
        out_shape=jax.ShapeDtypeStruct((groups, size, 2 * rows, width), F32),
        compiler_params=params(),
        cost_estimate=cost(size, 2, width),
        name="side_terms",
    )(own, lower, upper, before, after)


def own_again(first, green, scattered, begin, step):
    groups, size, double, width = first.shape
    return pl.pallas_call(
        functools.partial(terms_kernel, 1, load_rows, load_rows, store_matrix, step),
        grid=(size // step,),
        in_specs=[
            rows_spec(step, groups, double // 2, width),
            matrix_spec(step, begin // step, width, 1),
            rows_spec(step, groups, double // 2, width),
        ],
        out_specs=matrix_spec(step, 0, width, 0),
        out_shape=jax.ShapeDtypeStruct((size, 2, width, width), F32),
        compiler_params=params(),
        cost_estimate=cost(size, 1, width),
        name="own_again",
    )(first, green, scattered)


def side_again_kernel(step, aliased, *refs):
    refs = refs[1:] if aliased else refs
    terms_kernel(2, load_matrix, load_rows, store_matrix, step, *refs)


def side_again(result, partial, lower, upper, before, after, begin, step):
    size, _, width, _ = partial.shape
    groups, _, double, _ = before.shape
    at = begin // step
    aliased = result is not None
    return pl.pallas_call(
        functools.partial(side_again_kernel, step, aliased),
        grid=(size // step,),
        in_specs=([pl.BlockSpec(memory_space=pl.ANY)] if aliased else [])
        + [matrix_spec(step, 0, width, 0)]
        + [matrix_spec(step, at, width, 1)] * 2
        + [rows_spec(step, groups, double // 2, width)] * 2,
        out_specs=matrix_spec(step, at, width, 1),
        out_shape=jax.ShapeDtypeStruct(lower.shape, F32),
        input_output_aliases={0: 0} if aliased else {},
        compiler_params=params(),
        cost_estimate=cost(size, 2, width),
        name="side_again",
    )(*([result] if aliased else []), partial, lower, upper, before, after)


def convolve_kernel(chunks, groups, rows, table_ref, mask_ref, weight_ref, *refs):
    count = len(chunks)
    inputs, outputs = refs[:count], refs[count:]
    total = table_ref.shape[1]
    width = weight_ref.shape[-1]
    stride = 2 * rows
    weight = weight_ref.reshape(total * stride, width)
    arrived = [ref.reshape(groups * size * stride, width) for ref, (_, size) in zip(inputs, chunks)]
    leaving = [ref.reshape(groups * size * stride, width) for ref, (_, size) in zip(outputs, chunks)]

    def apply(value):
        high, low = split(value)
        both = dot(table_ref[...], high)
        out = both[: 2 * total] + (both[2 * total :] + dot(table_ref[: 2 * total], low))
        return out[:total], out[total:]

    def one_row(row, carry):
        parts = []
        for p in (0, 1):
            pieces = [
                arrived[c][pl.ds(j * size * stride + p * rows + row, size, stride=stride), :]
                for j in range(groups)
                for c, (_, size) in enumerate(chunks)
            ]
            parts.append(jnp.concatenate(pieces, axis=0))
        cosine, sine = apply(jnp.concatenate(parts, axis=1))
        real = cosine[:, :width] + sine[:, width:]
        imag = cosine[:, width:] - sine[:, :width]
        weight_real = weight[pl.ds(row, total, stride=stride), :]
        weight_imag = weight[pl.ds(rows + row, total, stride=stride), :]
        cosine, sine = apply(
            jnp.concatenate([real * weight_real - imag * weight_imag, real * weight_imag + imag * weight_real], axis=1)
        )
        kept = mask_ref[pl.ds(row, 1), :] * (1.0 / total)
        results = (-(cosine[:, width:] + sine[:, :width]) * kept, (cosine[:, :width] - sine[:, width:]) * kept)
        for p in (0, 1):
            for j in range(groups):
                for c, (begin, size) in enumerate(chunks):
                    at = j * (total // groups) + begin
                    leaving[c][pl.ds(j * size * stride + p * rows + row, size, stride=stride), :] = results[p][at : at + size]
        return carry

    lax.fori_loop(0, rows, one_row, 0)


def convolve(arrived, weights, mask, chunks):
    groups, _, double, width = arrived[0].shape
    total = weights.shape[0]
    rows = double // 2
    phase = np.arange(total)[:, None] * np.arange(total)[None, :] % total
    angle = 2.0 * np.pi / total * phase
    table = np.concatenate([np.cos(angle), np.sin(angle)], axis=0).astype(np.float32)
    high = table.astype(jnp.bfloat16)
    low = (table - high.astype(np.float32)).astype(jnp.bfloat16)
    both = jnp.asarray(np.concatenate([high, low], axis=0))
    whole = pl.BlockSpec(memory_space=pltpu.VMEM)
    return pl.pallas_call(
        functools.partial(convolve_kernel, chunks, groups, rows),
        in_specs=[whole] * (3 + len(chunks)),
        out_specs=[whole] * len(chunks),
        out_shape=[jax.ShapeDtypeStruct(part.shape, F32) for part in arrived],
        compiler_params=params(),
        cost_estimate=pl.CostEstimate(
            flops=2 * 6 * 2 * total * total * 2 * rows * width, bytes_accessed=3 * total * double * width * 4, transcendentals=0
        ),
        name="convolve",
    )(both, mask, weights, *arrived)


def neighbours(value, count):
    up = [(i, i + 1) for i in range(count - 1)]
    down = [(i + 1, i) for i in range(count - 1)]
    return lax.ppermute(value, "slab", up), lax.ppermute(value, "slab", down)


def exchange(value):
    return lax.all_to_all(value, "energy", split_axis=0, concat_axis=0, tiled=True)


def local(green_diag, green_lower, green_upper, sigma_lesser, screened, pattern):
    groups = lax.axis_size("energy")
    slabs = lax.axis_size("slab")
    _, energies, _, width, _ = sigma_lesser.shape
    rows = width // groups
    total = screened.shape[1]
    step = 2
    parts = 4
    size = energies // parts
    chunks = [(at, size) for at in range(0, energies, size)]

    halos = [neighbours(sigma_lesser[:, at : at + size], slabs) for at, size in chunks]
    own = own_terms(green_diag, sigma_lesser, step)
    firsts = [
        side_terms(own, green_lower, green_upper, *halo, at, size, groups, step) for halo, (at, size) in zip(halos, chunks)
    ]
    arrived = [exchange(first) for first in firsts]

    kept = pattern[0].astype(F32)
    own_rows = lax.dynamic_slice_in_dim(kept, lax.axis_index("energy") * rows, rows)
    mask = own_rows[:, None] * kept[None, :]
    leaving = convolve(arrived, screened.reshape(total, 2 * rows, width), mask, chunks)

    scattered = [exchange(part) for part in leaving]
    halos = [neighbours(part, slabs) for part in scattered]
    partials = [own_again(first, green_diag, part, at, step) for first, part, (at, _) in zip(firsts, scattered, chunks)]
    result = None
    for partial, halo, (at, _) in zip(partials, halos, chunks):
        result = side_again(result, partial, green_lower, green_upper, *halo, at, step)
    return result


def solution(mesh):
    return jax.shard_map(
        local,
        mesh=mesh,
        in_specs=(
            P("slab", "energy", None, None, None),
            P("slab", "energy", None, None, None),
            P("slab", "energy", None, None, None),
            P("slab", "energy", None, None, None),
            P("slab", None, None, "energy", None),
            P("slab", None),
        ),
        out_specs=P("slab", "energy", None, None, None),
        check_vma=False,
    )
```

```python
import functools

import jax
import jax.numpy as jnp
import numpy as np
from jax import lax
from jax.experimental import pallas as pl
from jax.experimental.pallas import tpu as pltpu
from jax.sharding import PartitionSpec as P

F32 = jnp.float32
BF16 = jnp.bfloat16
MIB = 1024 * 1024


def params(mebibytes=16):
    return pltpu.CompilerParams(vmem_limit_bytes=mebibytes * MIB)


def split(value):
    high = value.astype(BF16)
    return high, (value - high.astype(F32)).astype(BF16)


def dot(first, second, transposed=False):
    dims = (((1,), (1,)), ((), ())) if transposed else (((1,), (0,)), ((), ()))
    return lax.dot_general(first, second, dims, preferred_element_type=F32)


def stack(*parts):
    return jnp.concatenate(parts, axis=0)


def beside(*parts):
    return jnp.concatenate(parts, axis=1)


def dot_stacked(first, second):
    rows = first.shape[0] // 2
    both = dot(first, second[0])
    return both[:rows] + (both[rows:] + dot(first[:rows], second[1]))


def sandwich(green, middle, turn):
    rows = green.shape[0] // 2
    first = dot_stacked(green, middle)
    out = dot(stack(*split(first), *split(turn(first))), green, transposed=True)
    real, real_low, imag, imag_low = (out[i * rows : (i + 1) * rows] for i in range(4))
    return beside(real[:, :rows] + (real[:, rows:] + real_low[:, :rows]), imag[:, :rows] + (imag[:, rows:] + imag_low[:, :rows]))


def turn_halves(value):
    width = value.shape[1] // 2
    return beside(value[:, width:], -value[:, :width])


def lane_of(value):
    return lax.broadcasted_iota(jnp.int32, value.shape, 1)


def turn_packed(value, extra):
    width = value.shape[1] // 2
    wide, narrow = value[:, :width], value[:, width:]
    lane = lane_of(wide)
    sign = jnp.where(lane < width // 2, 1.0, -1.0)
    wide = pltpu.roll(wide, width // 2, axis=1) * sign
    narrow = jnp.where(lane % (2 * extra) < extra, pltpu.roll(narrow, width - extra, axis=1), -pltpu.roll(narrow, extra, axis=1))
    return beside(wide, narrow)


def load_matrix(ref, index):
    lead = (0,) * (len(ref.shape) - 4)
    return beside(ref[lead + (index, 0)], ref[lead + (index, 1)])


def load_flat(ref, index):
    width = ref.shape[1]
    at = 2 * index * width
    return beside(ref[at : at + width, :], ref[at + width : at + 2 * width, :])


def load_rows(ref, index):
    groups, _, double, _ = ref.shape
    rows = double // 2
    return beside(*[stack(*[ref[r, index, p * rows : (p + 1) * rows, :] for r in range(groups)]) for p in (0, 1)])


def store_matrix(ref, index, value):
    width = value.shape[1] // 2
    lead = (0,) * (len(ref.shape) - 4)
    ref[lead + (index, 0)] = value[:, :width]
    ref[lead + (index, 1)] = value[:, width:]


def store_rows(ref, index, value):
    groups, _, double, width = ref.shape
    rows = double // 2
    for r in range(groups):
        for p in (0, 1):
            ref[r, index, p * rows : (p + 1) * rows, :] = value[r * rows : (r + 1) * rows, p * width : (p + 1) * width]


def whole_term(green, middle):
    pairs = [stack(part, beside(-part[:, part.shape[1] // 2 :], part[:, : part.shape[1] // 2])) for part in split(middle)]
    return sandwich(stack(*split(green)), pairs, turn_halves)


def packed_term(green, middle_ref, index, size, extra):
    width = green.shape[1] // 2
    share = width // (2 * extra)
    middle = beside(middle_ref[index], middle_ref[size + index // share])
    pairs = []
    for part, turned in zip(split(middle), split(-turn_packed(middle, extra))):
        half = width // 2
        pairs.append(stack(part[:half], turned[:half], *([part[half:], turned[half:]] * share)))
    return sandwich(green, pairs, functools.partial(turn_packed, extra=extra))


def matrix_spec(step, offset, width, lead):
    shape = (1,) * lead + (step, 2, width, width)
    return pl.BlockSpec(shape, lambda i: (0,) * lead + (i + offset, 0, 0, 0))


def flat_spec(step, width):
    return pl.BlockSpec((2 * step * width, width), lambda i: (i, 0))


def rows_spec(step, groups, rows, width):
    return pl.BlockSpec((groups, step, 2 * rows, width), lambda i: (0, i, 0, 0))


def in_any():
    return pl.BlockSpec(memory_space=pl.ANY)


def cost(energies, count, width):
    return pl.CostEstimate(
        flops=energies * count * width**2,
        bytes_accessed=energies * count * width,
        transcendentals=0,
    )


def own_terms_kernel(step, green, sigma, out):
    for index in range(step):
        store_matrix(out, index, whole_term(load_matrix(green, index), load_matrix(sigma, index)))


def own_terms(green, sigma, step):
    _, energies, _, width, _ = green.shape
    return pl.pallas_call(
        functools.partial(own_terms_kernel, step),
        grid=(energies // step,),
        in_specs=[matrix_spec(step, 0, width, 1)] * 2,
        out_specs=matrix_spec(step, 0, width, 0),
        out_shape=jax.ShapeDtypeStruct((energies, 2, width, width), F32),
        compiler_params=params(60),
        cost_estimate=cost(energies, 1, width),
        name="own_terms",
    )(green, sigma)


def side_terms_kernel(step, total, lower, upper, before, after, out, send):
    for index in range(step):
        value = load_matrix(total, index)
        value = value + whole_term(load_matrix(lower, index), load_flat(before, index))
        value = value + whole_term(load_matrix(upper, index), load_flat(after, index))
        store_matrix(out, index, value)
        store_rows(send, index, value)


def side_terms(total, lower, upper, before, after, begin, size, groups, step):
    width = total.shape[-1]
    rows = width // groups
    at = begin // step
    return pl.pallas_call(
        functools.partial(side_terms_kernel, step),
        grid=(size // step,),
        in_specs=[matrix_spec(step, at, width, 0)] + [matrix_spec(step, at, width, 1)] * 2 + [flat_spec(step, width)] * 2,
        out_specs=[matrix_spec(step, 0, width, 0), rows_spec(step, groups, rows, width)],
        out_shape=[
            jax.ShapeDtypeStruct((size, 2, width, width), F32),
            jax.ShapeDtypeStruct((groups, size, 2 * rows, width), F32),
        ],
        compiler_params=params(60),
        cost_estimate=cost(size, 2, width),
        name="side_terms",
    )(total, lower, upper, before, after)


def whole_again_kernel(step, count, aliased, *refs):
    refs = refs[1:] if aliased else refs
    base, greens, middles, out = refs[0], refs[1 : 1 + count], refs[1 + count : 1 + 2 * count], refs[-1]
    for index in range(step):
        value = load_matrix(base, index)
        for green, middle in zip(greens, middles):
            value = value + whole_term(load_matrix(green, index), load_rows(middle, index))
        store_matrix(out, index, value)


def whole_again(result, base, base_begin, greens, middles, begin, step, shape):
    groups, size, double, width = middles[0].shape
    count = len(greens)
    at = begin // step
    aliased = result is not None
    return pl.pallas_call(
        functools.partial(whole_again_kernel, step, count, aliased),
        grid=(size // step,),
        in_specs=[in_any()] * aliased
        + [matrix_spec(step, base_begin // step, width, 0)]
        + [matrix_spec(step, at, width, 1)] * count
        + [rows_spec(step, groups, double // 2, width)] * count,
        out_specs=matrix_spec(step, at if len(shape) == 5 else 0, width, len(shape) - 4),
        out_shape=jax.ShapeDtypeStruct(shape, F32),
        input_output_aliases={0: 0} if aliased else {},
        compiler_params=params(),
        cost_estimate=cost(size, count, width),
        name="whole_again",
    )(*([result] * aliased), base, *greens, *middles)


def packed_again_kernel(step, bases, count, size, extra, aliased, *refs):
    refs = refs[1:] if aliased else refs
    base_refs, refs = refs[: len(bases)], refs[len(bases) :]
    greens, middles, out = refs[:count], refs[count : 2 * count], refs[-1]
    here = pl.program_id(0)
    for index in range(step):
        value = load_matrix(base_refs[0], index)
        for (begin, _), ref in zip(bases[1:], base_refs[1:]):
            value = jnp.where(here >= begin, load_matrix(ref, index), value)
        for green, middle in zip(greens, middles):
            value = value + packed_term(green[index], middle, here * step + index, size, extra)
        store_matrix(out, index, value)


def packed_again(result, bases, greens, middles, begin, size, step, shape, extra):
    span, cap, width = middles[0].shape
    count = len(greens)
    at = begin // step
    aliased = result is not None
    places = chunks_of([base.shape[0] // step for base in bases])
    specs = [
        pl.BlockSpec((step, 2, width, width), lambda i, start=start, steps=steps: (jnp.clip(i - start, 0, steps - 1), 0, 0, 0))
        for start, steps in places
    ]
    return pl.pallas_call(
        functools.partial(packed_again_kernel, step, places, count, size, extra, aliased),
        grid=(size // step,),
        in_specs=[in_any()] * aliased
        + specs
        + [pl.BlockSpec((step, 2 * width, 2 * width), lambda i: (i + at, 0, 0))] * count
        + [pl.BlockSpec((span, cap, width), lambda i: (0, 0, 0))] * count,
        out_specs=matrix_spec(step, at if len(shape) == 5 else 0, width, len(shape) - 4),
        out_shape=jax.ShapeDtypeStruct(shape, F32),
        input_output_aliases={0: 0} if aliased else {},
        compiler_params=params(),
        cost_estimate=cost(size, count, width),
        name="packed_again",
    )(*([result] * aliased), *bases, *greens, *middles)


def pack_green_kernel(step, extra, place, *refs):
    count = len(refs) // 2
    width = place.shape[1] // 2
    share = width // (2 * extra)
    for green, out, which in zip(refs[:count], refs[count:], range(count)):
        for index in range(step):
            both = dot(stack(*split(load_matrix(green, index))), place[which])
            lane = lane_of(both) - width
            other = (lane >= 0) & (lane // (2 * extra) != index % share)
            out[index] = jnp.where(other, 0.0, both).astype(BF16)


def pack_green(greens, places, step, extra):
    _, energies, _, width, _ = greens[0].shape
    count = len(greens)
    return pl.pallas_call(
        functools.partial(pack_green_kernel, step, extra),
        grid=(energies // step,),
        in_specs=[pl.BlockSpec(places.shape, lambda i: (0, 0, 0))] + [matrix_spec(step, 0, width, 1)] * count,
        out_specs=[pl.BlockSpec((step, 2 * width, 2 * width), lambda i: (i, 0, 0))] * count,
        out_shape=[jax.ShapeDtypeStruct((energies, 2 * width, 2 * width), BF16)] * count,
        compiler_params=params(60),
        cost_estimate=pl.CostEstimate(
            flops=count * energies * 16 * width**3, bytes_accessed=count * energies * 16 * width**2, transcendentals=0
        ),
        name="pack_green",
    )(places, *greens)


def pack_rows_kernel(rows, chosen, part, out):
    groups, _, _ = part.shape
    for at in range(out.shape[0]):
        block = stack(*[part[r, at * rows : (at + 1) * rows, :] for r in range(groups)])
        high, low = split(block)
        out[at] = dot(chosen[...], high) + dot(chosen[...], low)


def pack_rows(chosen, part, rows):
    groups, height, width = part.shape
    cap = chosen.shape[0]
    whole = pl.BlockSpec(memory_space=pltpu.VMEM)
    return pl.pallas_call(
        functools.partial(pack_rows_kernel, rows),
        in_specs=[whole, whole],
        out_specs=whole,
        out_shape=jax.ShapeDtypeStruct((height // rows, cap, width), F32),
        compiler_params=params(),
        cost_estimate=pl.CostEstimate(
            flops=height // rows * 4 * cap * width**2, bytes_accessed=2 * groups * height * width * 4, transcendentals=0
        ),
        name="pack_rows",
    )(chosen, part)


def apply_table(table, value, size):
    both = dot(table, value[0])
    return both[:size] + (both[size:] + dot(table[:size], value[1]))


def forward_kernel(first, groups, rows, tables, weight_ref, *refs):
    inputs, out = refs[: len(first)], refs[-1]
    total, double, width = weight_ref.shape
    half = total // 2
    weight = weight_ref.reshape(total * double, width)
    arrived = [ref.reshape(groups * size * double, width) for ref, (_, size) in zip(inputs, first)]

    def load(row, p):
        pieces = [
            arrived[c][pl.ds(j * size * double + p * rows + row, size, stride=double), :]
            for j in range(groups)
            for c, (_, size) in enumerate(first)
        ]
        return stack(*pieces)

    def two_rows(pair, carry):
        at = (2 * pair, 2 * pair + 1)
        values = [[load(row, p) for row in at] for p in (0, 1)]
        for odd in (0, 1):
            sign = 1.0 - 2.0 * odd
            folded = [beside(*[value[:half] + sign * value[half:] for value in part]) for part in values]
            spectrum = apply_table(tables[odd], split(stack(*folded)), total)
            real, imag = spectrum[:half], spectrum[half:]
            weights = [
                beside(*[weight[pl.ds(odd * double + p * rows + row, half, stride=2 * double), :] for row in at]) for p in (0, 1)
            ]
            weighed = split(stack(real * weights[0] - imag * weights[1], real * weights[1] + imag * weights[0]))
            for part in (0, 1):
                out[pair, odd, part] = weighed[part]
        return carry

    lax.fori_loop(0, rows // 2, two_rows, 0)


def forward(arrived, weights, first):
    groups, _, double, width = arrived[0].shape
    total = weights.shape[0]
    whole = pl.BlockSpec(memory_space=pltpu.VMEM)
    shape = (double // 4, 2, 2, total, 2 * width)
    return pl.pallas_call(
        functools.partial(forward_kernel, first, groups, double // 2),
        in_specs=[whole] * (2 + len(first)),
        out_specs=whole,
        out_shape=jax.ShapeDtypeStruct(shape, BF16),
        compiler_params=params(60),
        cost_estimate=pl.CostEstimate(
            flops=6 * total * total * double * width, bytes_accessed=3 * total * double * width * 4, transcendentals=0
        ),
        name="forward",
    )(transform_tables(total, None), weights, *arrived)


def backward_kernel(size, groups, extra, tables, weighed, final_ref, out_ref, *scratch):
    pairs, _, _, total, double = weighed.shape
    width = double // 2
    rows = 2 * pairs
    count = groups * size
    share = width // (2 * extra) if extra else 0
    span = (size + size // share) * rows if extra else size * 2 * rows
    out = out_ref.reshape(groups * span, width)

    def store_whole(row, real, imag):
        kept = final_ref[pl.ds(row, 1), :] * (1.0 / total)
        for p, value in enumerate((-imag * kept, real * kept)):
            for j in range(groups):
                out[pl.ds(j * span + p * rows + row, size, stride=2 * rows), :] = value[j * size : (j + 1) * size]

    def store_packed(row, real, imag):
        value = beside(-imag, real) * (1.0 / total)
        both = dot(stack(*split(value)), final_ref[...])
        both = both[:count] + both[count:]
        scratch[0][...] = both[:, width:]
        quarter = [scratch[0][pl.ds(q, count // share, stride=share), :] for q in range(share)]
        lane = lane_of(quarter[0]) // (2 * extra)
        narrow = quarter[0]
        for q in range(1, share):
            narrow = jnp.where(lane == q, quarter[q], narrow)
        for j in range(groups):
            out[pl.ds(j * span + row, size, stride=rows), :] = both[j * size : (j + 1) * size, :width]
            short = size // share
            out[pl.ds(j * span + size * rows + row, short, stride=rows), :] = narrow[j * short : (j + 1) * short]

    def two_rows(pair, carry):
        backs = [apply_table(tables[odd], (weighed[pair, odd, 0], weighed[pair, odd, 1]), count) for odd in (0, 1)]
        early, late = backs[0] + backs[1], backs[0] - backs[1]
        for index in (0, 1):
            lanes = slice(index * width, (index + 1) * width)
            real = stack(early[: count // 2, lanes], late[: count // 2, lanes])
            imag = stack(early[count // 2 :, lanes], late[count // 2 :, lanes])
            (store_packed if extra else store_whole)(2 * pair + index, real, imag)
        return carry

    lax.fori_loop(0, pairs, two_rows, 0)


def backward(weighed, final, begin, size, groups, extra):
    pairs, _, _, total, double = weighed.shape
    width = double // 2
    rows = 2 * pairs
    local = total // groups
    chosen = [j * local + begin + l for j in range(groups // 2) for l in range(size)]
    if extra:
        share = width // (2 * extra)
        shape = (groups, (size + size // share) * rows, width)
        scratch = [pltpu.VMEM((groups * size, width), F32)]
    else:
        shape = (groups, size, 2 * rows, width)
        scratch = []
    whole = pl.BlockSpec(memory_space=pltpu.VMEM)
    return pl.pallas_call(
        functools.partial(backward_kernel, size, groups, extra),
        in_specs=[whole] * 3,
        out_specs=whole,
        out_shape=jax.ShapeDtypeStruct(shape, F32),
        scratch_shapes=scratch,
        compiler_params=params(28),
        cost_estimate=pl.CostEstimate(
            flops=6 * total * groups * size * 2 * rows * width,
            bytes_accessed=(total + groups * size) * 2 * rows * width * 4,
            transcendentals=0,
        ),
        name="backward",
    )(transform_tables(total, chosen), weighed, final)


def transform_tables(total, chosen):
    half = total // 2
    tables = []
    for odd in (0, 1):
        phase = (2 * np.arange(half)[:, None] + odd) * np.arange(half)[None, :] % total
        cosine, sine = np.cos(2.0 * np.pi / total * phase), np.sin(2.0 * np.pi / total * phase)
        if chosen is None:
            table = np.block([[cosine, sine], [-sine, cosine]])
        else:
            cosine, sine = cosine.T[chosen], sine.T[chosen]
            table = np.block([[cosine, -sine], [sine, cosine]])
        tables.append(table.astype(np.float32))
    high = [table.astype(jnp.bfloat16) for table in tables]
    low = [(table - part.astype(np.float32)).astype(jnp.bfloat16) for table, part in zip(tables, high)]
    return jnp.asarray(np.stack([np.concatenate(parts, axis=0) for parts in zip(high, low)]))


def neighbours(value, count):
    up = [(i, i + 1) for i in range(count - 1)]
    down = [(i + 1, i) for i in range(count - 1)]
    return lax.ppermute(value, "slab", up), lax.ppermute(value, "slab", down)


def exchange(value):
    return lax.all_to_all(value, "energy", split_axis=0, concat_axis=0, tiled=True)


def tied(value, earlier):
    return lax.optimization_barrier((value, earlier))[0]


def chunks_of(sizes):
    return [(sum(sizes[:i]), size) for i, size in enumerate(sizes)]


def placement(pattern, rank, extra):
    width = pattern.shape[0]
    lane = jnp.arange(2 * width)
    narrow = lane - width
    imag = jnp.where(lane < width, lane // (width // 2), narrow % (2 * extra) // extra)
    slot = jnp.where(lane < width, lane % (width // 2), width // 2 + narrow % extra)
    source = jnp.arange(2 * width)
    hit = (source[:, None] // width == imag[None, :]) & (jnp.tile(rank, 2)[:, None] == slot[None, :])
    return (hit & (jnp.tile(pattern, 2)[:, None] > 0)).astype(BF16)


def local(green_diag, green_lower, green_upper, sigma_lesser, screened, pattern):
    groups = lax.axis_size("energy")
    slabs = lax.axis_size("slab")
    _, energies, _, width, _ = sigma_lesser.shape
    rows = width // groups
    total = screened.shape[1]
    step = 4
    extra = width // 8
    cap = width // 2 + extra
    first = chunks_of([energies // 4] * 4)
    second = chunks_of([energies // 2] + [energies // 4] * 2)

    mine = pattern[0].astype(F32)
    sent = [sigma_lesser[0, at : at + size].reshape(2 * size * width, width) for at, size in first]
    edge = sent[0].shape[0]
    sent[0] = stack(sent[0], jnp.broadcast_to(mine, (8, width)))
    own = own_terms(green_diag, sigma_lesser, step)
    halos, bases, arrived = [neighbours(part, slabs) for part in sent[:2]], [], []
    patterns = jnp.stack([mine, halos[0][0][edge], halos[0][1][edge]])
    ranks = jnp.cumsum(patterns, axis=1).astype(jnp.int32) - 1
    places = jnp.stack([placement(patterns[side], ranks[side], extra) for side in range(3)])
    packed_greens = pack_green([green_diag, green_lower, green_upper], places, step, extra)
    for index, (at, size) in enumerate(first):
        if index + 2 < len(first):
            halos.append(neighbours(tied(sent[index + 2], (halos[index], own)), slabs))
        halo = halos[index]
        if index:
            halo = tied(halo, (arrived[max(index - 2, 0)], packed_greens))
        base, send = side_terms(own, green_lower, green_upper, *halo, at, size, groups, step)
        bases.append(base)
        arrived.append(exchange(send))

    fits = lax.pmax(tied(jnp.sum(mine), bases[-1]), "slab") <= cap
    chosen = ((ranks[0][None, :] == jnp.arange(cap)[:, None]) & (mine[None, :] > 0)).astype(BF16)
    own_rows = lax.dynamic_slice_in_dim(mine, lax.axis_index("energy") * rows, rows)
    mask = own_rows[:, None] * mine[None, :]
    weighed = forward(arrived, screened.reshape(total, 2 * rows, width), first)

    def within(begin, size):
        return [base for base, (at, _) in zip(bases, first) if begin <= at < begin + size]

    def packed_rest(weighed):
        packed, halos = [], []
        parts = [backward(weighed, places[0], at, size, groups, extra) for at, size in second]
        for index, part in enumerate(parts):
            part = exchange(tied(part, packed[-1]) if index else part)
            packed.append(pack_rows(chosen, part if index else tied(part, parts), rows))
            halos.append(neighbours(packed[-1], slabs))
        partials = [
            packed_again(None, within(at, size), packed_greens[:1], [part], at, size, step, (size, 2, width, width), extra)
            for part, (at, size) in zip(packed, second)
        ]
        result = None
        for partial, halo, (at, size) in zip(partials, halos, second):
            result = packed_again(result, [partial], packed_greens[1:], halo, at, size, step, green_lower.shape, extra)
        return result

    def whole_rest(weighed):
        base = jnp.concatenate(bases, axis=0)
        middles = [exchange(backward(weighed, mask, at, size, groups, 0)) for at, size in second]
        halos = [neighbours(part, slabs) for part in middles]
        partials = [
            whole_again(None, base, at, [green_diag], [part], at, step, (size, 2, width, width))
            for part, (at, size) in zip(middles, second)
        ]
        result = None
        for partial, halo, (at, _) in zip(partials, halos, second):
            result = whole_again(result, partial, 0, [green_lower, green_upper], halo, at, step, green_lower.shape)
        return result

    return lax.cond(fits, packed_rest, whole_rest, weighed)


def solution(mesh):
    return jax.shard_map(
        local,
        mesh=mesh,
        in_specs=(
            P("slab", "energy", None, None, None),
            P("slab", "energy", None, None, None),
            P("slab", "energy", None, None, None),
            P("slab", "energy", None, None, None),
            P("slab", None, None, "energy", None),
            P("slab", None),
        ),
        out_specs=P("slab", "energy", None, None, None),
        check_vma=False,
    )
```

```python
import functools

import jax
import jax.numpy as jnp
import numpy as np
from jax import lax
from jax.experimental import pallas as pl
from jax.experimental.pallas import tpu as pltpu
from jax.sharding import PartitionSpec as P

F32 = jnp.float32
BF16 = jnp.bfloat16
MIB = 1024 * 1024
UNROLL = 2


def params(mebibytes=16):
    return pltpu.CompilerParams(vmem_limit_bytes=mebibytes * MIB)


def split(value):
    high = value.astype(BF16)
    return high, (value - high.astype(F32)).astype(BF16)


def dot(first, second, transposed=False):
    dims = (((1,), (1,)), ((), ())) if transposed else (((1,), (0,)), ((), ()))
    return lax.dot_general(first, second, dims, preferred_element_type=F32)


def stack(*parts):
    return jnp.concatenate(parts, axis=0)


def beside(*parts):
    return jnp.concatenate(parts, axis=1)


def dot_stacked(first, second):
    rows = first.shape[0] // 2
    both = dot(first, second[0])
    return both[:rows] + (both[rows:] + dot(first[:rows], second[1]))


def sandwich(green, middle):
    rows = green.shape[0] // 2
    first = dot_stacked(green, middle)
    out = dot(stack(*split(first), *split(turn_halves(first))), green, transposed=True)
    real, real_low, imag, imag_low = (out[i * rows : (i + 1) * rows] for i in range(4))
    return beside(real[:, :rows] + (real[:, rows:] + real_low[:, :rows]), imag[:, :rows] + (imag[:, rows:] + imag_low[:, :rows]))


def turn_halves(value):
    width = value.shape[1] // 2
    return beside(value[:, width:], -value[:, :width])


def packed_sandwich(green, middle, turned, spread):
    rows, inner = green.shape[0] // 2, middle[0].shape[0]
    out = dot(stack(*middle, *turned), green, transposed=True)
    real, real_low, imag, imag_low = (out[i * inner : (i + 1) * inner] for i in range(4))
    inside = beside(real[:, :rows] + (real[:, rows:] + real_low[:, :rows]), imag[:, :rows] + (imag[:, rows:] + imag_low[:, :rows]))
    high, low = (spread(part, beside(-part[:, rows:], part[:, :rows])) for part in split(inside))
    both = dot(green, high)
    return both[:rows] + (both[rows:] + dot(green[:rows], low))


def lane_of(value):
    return lax.broadcasted_iota(jnp.int32, value.shape, 1)


def turn_packed(value, extra):
    width = value.shape[1] // 2
    wide, narrow = value[:, :width], value[:, width:]
    lane = lane_of(wide)
    sign = jnp.where(lane < width // 2, 1.0, -1.0)
    wide = pltpu.roll(wide, width // 2, axis=1) * sign
    narrow = jnp.where(lane % (2 * extra) < extra, pltpu.roll(narrow, width - extra, axis=1), -pltpu.roll(narrow, extra, axis=1))
    return beside(wide, narrow)


def load_matrix(ref, index):
    lead = (0,) * (len(ref.shape) - 4)
    return beside(ref[lead + (index, 0)], ref[lead + (index, 1)])


def load_flat(ref, index):
    width = ref.shape[1]
    at = 2 * index * width
    return beside(ref[at : at + width, :], ref[at + width : at + 2 * width, :])


def load_rows(ref, index):
    groups, _, double, _ = ref.shape
    rows = double // 2
    return beside(*[stack(*[ref[r, index, p * rows : (p + 1) * rows, :] for r in range(groups)]) for p in (0, 1)])


def store_matrix(ref, index, value):
    width = value.shape[1] // 2
    lead = (0,) * (len(ref.shape) - 4)
    ref[lead + (index, 0)] = value[:, :width]
    ref[lead + (index, 1)] = value[:, width:]


def store_rows(ref, index, value):
    groups, _, double, width = ref.shape
    rows = double // 2
    for r in range(groups):
        for p in (0, 1):
            ref[r, index, p * rows : (p + 1) * rows, :] = value[r * rows : (r + 1) * rows, p * width : (p + 1) * width]


def whole_term(green, middle):
    pairs = [stack(part, beside(-part[:, part.shape[1] // 2 :], part[:, : part.shape[1] // 2])) for part in split(middle)]
    return sandwich(stack(*split(green)), pairs)


def packed_term(green, middle_ref, index, size, extra):
    half = green.shape[1] // 4
    share = half // extra
    middle = beside(middle_ref[index], middle_ref[size + index // share])

    def spread(part, turned):
        return stack(part[:half], turned[:half], *([part[half:], turned[half:]] * share))

    return packed_sandwich(green, split(middle), split(turn_packed(middle, extra)), spread)


def matrix_spec(step, offset, width, lead):
    shape = (1,) * lead + (step, 2, width, width)
    return pl.BlockSpec(shape, lambda i: (0,) * lead + (i + offset, 0, 0, 0))


def flat_spec(step, width):
    return pl.BlockSpec((2 * step * width, width), lambda i: (i, 0))


def rows_spec(step, groups, rows, width):
    return pl.BlockSpec((groups, step, 2 * rows, width), lambda i: (0, i, 0, 0))


def in_any():
    return pl.BlockSpec(memory_space=pl.ANY)


def cost(micros):
    return pl.CostEstimate(flops=int(micros * 0.3 * 1.15e9), bytes_accessed=int(micros * 0.3 * 3.69e6), transcendentals=0)


def own_terms_kernel(step, green, sigma, out):
    for index in range(step):
        store_matrix(out, index, whole_term(load_matrix(green, index), load_matrix(sigma, index)))


def own_terms(green, sigma, step):
    _, energies, _, width, _ = green.shape
    return pl.pallas_call(
        functools.partial(own_terms_kernel, step),
        grid=(energies // step,),
        in_specs=[matrix_spec(step, 0, width, 1)] * 2,
        out_specs=matrix_spec(step, 0, width, 0),
        out_shape=jax.ShapeDtypeStruct((energies, 2, width, width), F32),
        compiler_params=params(60),
        cost_estimate=cost(0.35 * energies),
        name="own_terms",
    )(green, sigma)


def side_terms_kernel(step, total, lower, upper, before, after, out, send):
    for index in range(step):
        value = load_matrix(total, index)
        value = value + whole_term(load_matrix(lower, index), load_flat(before, index))
        value = value + whole_term(load_matrix(upper, index), load_flat(after, index))
        store_matrix(out, index, value)
        store_rows(send, index, value)


def side_terms(total, lower, upper, before, after, begin, size, groups, step):
    width = total.shape[-1]
    rows = width // groups
    at = begin // step
    return pl.pallas_call(
        functools.partial(side_terms_kernel, step),
        grid=(size // step,),
        in_specs=[matrix_spec(step, at, width, 0)] + [matrix_spec(step, at, width, 1)] * 2 + [flat_spec(step, width)] * 2,
        out_specs=[matrix_spec(step, 0, width, 0), rows_spec(step, groups, rows, width)],
        out_shape=[
            jax.ShapeDtypeStruct((size, 2, width, width), F32),
            jax.ShapeDtypeStruct((groups, size, 2 * rows, width), F32),
        ],
        compiler_params=params(60),
        cost_estimate=cost(0.75 * size),
        name="side_terms",
    )(total, lower, upper, before, after)


def whole_again_kernel(step, count, aliased, *refs):
    refs = refs[1:] if aliased else refs
    base, greens, middles, out = refs[0], refs[1 : 1 + count], refs[1 + count : 1 + 2 * count], refs[-1]
    for index in range(step):
        value = load_matrix(base, index)
        for green, middle in zip(greens, middles):
            value = value + whole_term(load_matrix(green, index), load_rows(middle, index))
        store_matrix(out, index, value)


def whole_again(result, base, base_begin, greens, middles, begin, step, shape):
    groups, size, double, width = middles[0].shape
    count = len(greens)
    at = begin // step
    aliased = result is not None
    return pl.pallas_call(
        functools.partial(whole_again_kernel, step, count, aliased),
        grid=(size // step,),
        in_specs=[in_any()] * aliased
        + [matrix_spec(step, base_begin // step, width, 0)]
        + [matrix_spec(step, at, width, 1)] * count
        + [rows_spec(step, groups, double // 2, width)] * count,
        out_specs=matrix_spec(step, at if len(shape) == 5 else 0, width, len(shape) - 4),
        out_shape=jax.ShapeDtypeStruct(shape, F32),
        input_output_aliases={0: 0} if aliased else {},
        compiler_params=params(),
        cost_estimate=cost(0.3 * count * size),
        name="whole_again",
    )(*([result] * aliased), base, *greens, *middles)


def packed_again_kernel(step, bases, count, size, extra, aliased, *refs):
    refs = refs[1:] if aliased else refs
    base_refs, refs = refs[: len(bases)], refs[len(bases) :]
    greens, middles, out = refs[:count], refs[count : 2 * count], refs[-1]
    here = pl.program_id(0)
    for index in range(step):
        value = load_matrix(base_refs[0], index)
        for (begin, _), ref in zip(bases[1:], base_refs[1:]):
            value = jnp.where(here >= begin, load_matrix(ref, index), value)
        for green, middle in zip(greens, middles):
            value = value + packed_term(green[index], middle, here * step + index, size, extra)
        store_matrix(out, index, value)


def packed_again(result, bases, greens, middles, begin, size, step, shape, extra):
    span, cap, width = middles[0].shape
    count = len(greens)
    at = begin // step
    aliased = result is not None
    places = chunks_of([base.shape[0] // step for base in bases])
    specs = [
        pl.BlockSpec((step, 2, width, width), lambda i, start=start, steps=steps: (jnp.clip(i - start, 0, steps - 1), 0, 0, 0))
        for start, steps in places
    ]
    return pl.pallas_call(
        functools.partial(packed_again_kernel, step, places, count, size, extra, aliased),
        grid=(size // step,),
        in_specs=[in_any()] * aliased
        + specs
        + [pl.BlockSpec((step, 2 * width, 2 * width), lambda i: (i + at, 0, 0))] * count
        + [pl.BlockSpec((span, cap, width), lambda i: (0, 0, 0))] * count,
        out_specs=matrix_spec(step, at if len(shape) == 5 else 0, width, len(shape) - 4),
        out_shape=jax.ShapeDtypeStruct(shape, F32),
        input_output_aliases={0: 0} if aliased else {},
        compiler_params=params(),
        cost_estimate=cost(0.3 * count * size),
        name="packed_again",
    )(*([result] * aliased), *bases, *greens, *middles)


def pack_green_kernel(step, extra, place, *refs):
    count = len(refs) // 2
    width = place.shape[1] // 2
    share = width // (2 * extra)
    for green, out, which in zip(refs[:count], refs[count:], range(count)):
        for index in range(step):
            both = dot(stack(*split(load_matrix(green, index))), place[which])
            lane = lane_of(both) - width
            other = (lane >= 0) & (lane // (2 * extra) != index % share)
            out[index] = jnp.where(other, 0.0, both).astype(BF16)


def pack_green(greens, places, step, extra):
    _, energies, _, width, _ = greens[0].shape
    count = len(greens)
    return pl.pallas_call(
        functools.partial(pack_green_kernel, step, extra),
        grid=(energies // step,),
        in_specs=[pl.BlockSpec(places.shape, lambda i: (0, 0, 0))] + [matrix_spec(step, 0, width, 1)] * count,
        out_specs=[pl.BlockSpec((step, 2 * width, 2 * width), lambda i: (i, 0, 0))] * count,
        out_shape=[jax.ShapeDtypeStruct((energies, 2 * width, 2 * width), BF16)] * count,
        compiler_params=params(60),
        cost_estimate=cost(0.13 * count * energies),
        name="pack_green",
    )(places, *greens)


def pack_rows_kernel(rows, chosen, part, out):
    groups, _, _ = part.shape
    for at in range(out.shape[0]):
        block = stack(*[part[r, at * rows : (at + 1) * rows, :] for r in range(groups)])
        high, low = split(block)
        out[at] = dot(chosen[...], high) + dot(chosen[...], low)


def pack_rows(chosen, part, rows):
    groups, height, width = part.shape
    cap = chosen.shape[0]
    whole = pl.BlockSpec(memory_space=pltpu.VMEM)
    return pl.pallas_call(
        functools.partial(pack_rows_kernel, rows),
        in_specs=[whole, whole],
        out_specs=whole,
        out_shape=jax.ShapeDtypeStruct((height // rows, cap, width), F32),
        compiler_params=params(),
        cost_estimate=cost(1.5),
        name="pack_rows",
    )(chosen, part)


def apply_table(table, value, size):
    both = dot(table, value[0])
    return both[:size] + (both[size:] + dot(table[:size], value[1]))


def convolve_kernel(first, second, groups, rows, extra, forth, back, weight_ref, final_ref, *refs):
    inputs, outputs, scratch = refs[: len(first)], refs[len(first) : len(first) + len(second)], refs[len(first) + len(second) :]
    total, double, width = weight_ref.shape
    half = total // 2
    local = total // groups
    share = width // (2 * extra) if extra else 0
    weight = weight_ref.reshape(total * double, width)
    arrived = [ref.reshape(groups * size * double, width) for ref, (_, size) in zip(inputs, first)]
    spans = [(size + size // share) * rows if extra else size * double for _, size in second]
    leaving = [ref.reshape(groups * span, width) for ref, span in zip(outputs, spans)]

    def load(row, p):
        pieces = [
            arrived[c][pl.ds(j * size * double + p * rows + row, size, stride=double), :]
            for j in range(groups)
            for c, (_, size) in enumerate(first)
        ]
        return stack(*pieces)

    def store_whole(row, real, imag):
        kept = final_ref[pl.ds(row, 1), :] * (1.0 / total)
        for p, value in enumerate((-imag * kept, real * kept)):
            for j in range(groups):
                for c, (begin, size) in enumerate(second):
                    at = j * local + begin
                    leaving[c][pl.ds(j * spans[c] + p * rows + row, size, stride=double), :] = value[at : at + size]

    def store_packed(row, real, imag, spare):
        value = beside(-imag, real) * (1.0 / total)
        both = dot(stack(*split(value)), final_ref[...])
        both = both[:total] + both[total:]
        spare[...] = both[:, width:]
        quarter = [spare[pl.ds(q, total // share, stride=share), :] for q in range(share)]
        lane = lane_of(quarter[0]) // (2 * extra)
        narrow = quarter[0]
        for q in range(1, share):
            narrow = jnp.where(lane == q, quarter[q], narrow)
        for j in range(groups):
            for c, (begin, size) in enumerate(second):
                at = j * local + begin
                leaving[c][pl.ds(j * spans[c] + row, size, stride=rows), :] = both[at : at + size, :width]
                leaving[c][pl.ds(j * spans[c] + size * rows + row, size // share, stride=rows), :] = narrow[
                    at // share : (at + size) // share
                ]

    def two_rows(pair, carry):
        at = (2 * pair, 2 * pair + 1)
        values = [[load(row, p) for row in at] for p in (0, 1)]
        backs = []
        for odd in (0, 1):
            sign = 1.0 - 2.0 * odd
            folded = [beside(*[value[:half] + sign * value[half:] for value in part]) for part in values]
            spectrum = apply_table(forth[odd], split(stack(*folded)), total)
            real, imag = spectrum[:half], spectrum[half:]
            weights = [
                beside(*[weight[pl.ds(odd * double + p * rows + row, half, stride=2 * double), :] for row in at]) for p in (0, 1)
            ]
            weighed = split(stack(real * weights[0] - imag * weights[1], real * weights[1] + imag * weights[0]))
            backs.append(apply_table(back[odd], weighed, total))
        early, late = backs[0] + backs[1], backs[0] - backs[1]
        for index, row in enumerate(at):
            lanes = slice(index * width, (index + 1) * width)
            real = stack(early[:half, lanes], late[:half, lanes])
            imag = stack(early[half:, lanes], late[half:, lanes])
            if extra:
                store_packed(row, real, imag, scratch[index])
            else:
                store_whole(row, real, imag)
        return carry

    lax.fori_loop(0, rows // 2, two_rows, 0, unroll=UNROLL)


def convolve(arrived, weights, final, first, second, extra):
    groups, _, double, width = arrived[0].shape
    total = weights.shape[0]
    rows = double // 2
    if extra:
        share = width // (2 * extra)
        shapes = [(groups, (size + size // share) * rows, width) for _, size in second]
        scratch = [pltpu.VMEM((total, width), F32)] * 2
    else:
        shapes = [(groups, size, double, width) for _, size in second]
        scratch = []
    whole = pl.BlockSpec(memory_space=pltpu.VMEM)
    return pl.pallas_call(
        functools.partial(convolve_kernel, first, second, groups, rows, extra),
        in_specs=[whole] * (4 + len(first)),
        out_specs=[whole] * len(second),
        out_shape=[jax.ShapeDtypeStruct(shape, F32) for shape in shapes],
        scratch_shapes=scratch,
        compiler_params=params(60),
        cost_estimate=cost(0.3 * total / groups + 7.0),
        name="convolve",
    )(transform_tables(total, False), transform_tables(total, True), weights, final, *arrived)


def transform_tables(total, back):
    half = total // 2
    tables = []
    for odd in (0, 1):
        phase = (2 * np.arange(half)[:, None] + odd) * np.arange(half)[None, :] % total
        cosine, sine = np.cos(2.0 * np.pi / total * phase), np.sin(2.0 * np.pi / total * phase)
        table = np.block([[cosine, sine], [-sine, cosine]])
        tables.append((table.T if back else table).astype(np.float32))
    high = [table.astype(jnp.bfloat16) for table in tables]
    low = [(table - part.astype(np.float32)).astype(jnp.bfloat16) for table, part in zip(tables, high)]
    return jnp.asarray(np.stack([np.concatenate(parts, axis=0) for parts in zip(high, low)]))


def neighbours(value, count):
    up = [(i, i + 1) for i in range(count - 1)]
    down = [(i + 1, i) for i in range(count - 1)]
    return lax.ppermute(value, "slab", up), lax.ppermute(value, "slab", down)


def exchange(value):
    return lax.all_to_all(value, "energy", split_axis=0, concat_axis=0, tiled=True)


def tied(value, earlier):
    return lax.optimization_barrier((value, earlier))[0]


def chunks_of(sizes):
    return [(sum(sizes[:i]), size) for i, size in enumerate(sizes)]


def placement(pattern, rank, extra):
    width = pattern.shape[0]
    lane = jnp.arange(2 * width)
    narrow = lane - width
    imag = jnp.where(lane < width, lane // (width // 2), narrow % (2 * extra) // extra)
    slot = jnp.where(lane < width, lane % (width // 2), width // 2 + narrow % extra)
    source = jnp.arange(2 * width)
    hit = (source[:, None] // width == imag[None, :]) & (jnp.tile(rank, 2)[:, None] == slot[None, :])
    return (hit & (jnp.tile(pattern, 2)[:, None] > 0)).astype(BF16)


def local(green_diag, green_lower, green_upper, sigma_lesser, screened, pattern):
    groups = lax.axis_size("energy")
    slabs = lax.axis_size("slab")
    _, energies, _, width, _ = sigma_lesser.shape
    rows = width // groups
    total = screened.shape[1]
    step = 4
    extra = width // 8
    cap = width // 2 + extra
    first = chunks_of([energies // 4] * 4)
    second = chunks_of([energies // 2] * 2)

    mine = pattern[0].astype(F32)
    sent = [sigma_lesser[0, at : at + size].reshape(2 * size * width, width) for at, size in first]
    edge = sent[0].shape[0]
    sent[0] = stack(sent[0], jnp.broadcast_to(mine, (8, width)))
    own = own_terms(green_diag, sigma_lesser, 2 * step)
    halos, bases, arrived = [neighbours(part, slabs) for part in sent[:2]], [], []
    patterns = jnp.stack([mine, halos[0][0][edge], halos[0][1][edge]])
    ranks = jnp.cumsum(patterns, axis=1).astype(jnp.int32) - 1
    places = jnp.stack([placement(patterns[side], ranks[side], extra) for side in range(3)])
    packed_greens = pack_green([green_diag, green_lower, green_upper], places, step, extra)
    for index, (at, size) in enumerate(first):
        if index + 2 < len(first):
            halos.append(neighbours(tied(sent[index + 2], (halos[index], own)), slabs))
        halo = halos[index]
        if index:
            halo = tied(halo, (arrived[max(index - 2, 0)], packed_greens))
        base, send = side_terms(own, green_lower, green_upper, *halo, at, size, groups, step)
        bases.append(base)
        arrived.append(exchange(send))

    fits = lax.pmax(tied(jnp.sum(mine), bases[-1]), "slab") <= cap
    chosen = ((ranks[0][None, :] == jnp.arange(cap)[:, None]) & (mine[None, :] > 0)).astype(BF16)
    own_rows = lax.dynamic_slice_in_dim(mine, lax.axis_index("energy") * rows, rows)
    mask = own_rows[:, None] * mine[None, :]
    weights = screened.reshape(total, 2 * rows, width)
    parts = convolve(arrived, weights, places[0], first, second, extra)

    def within(begin, size):
        return [base for base, (at, _) in zip(bases, first) if begin <= at < begin + size]

    def packed_rest(parts, weights, *arrived):
        packed, halos, partials = [], [], []
        for index, (part, (at, size)) in enumerate(zip(parts, second)):
            part = exchange(tied(part, (packed[0], partials[: index - 1])) if index else part)
            packed.append(pack_rows(chosen, part, rows))
            halos.append(neighbours(packed[-1], slabs))
            partials.append(
                packed_again(
                    None, within(at, size), packed_greens[:1], packed[-1:], at, size, 2 * step, (size, 2, width, width), extra
                )
            )
        result = None
        for partial, halo, (at, size) in zip(partials, halos, second):
            result = packed_again(result, [partial], packed_greens[1:], halo, at, size, 2 * step, green_lower.shape, extra)
        return result

    def whole_rest(parts, weights, *arrived):
        base = jnp.concatenate(bases, axis=0)
        middles = [exchange(part) for part in convolve(arrived, weights, mask, first, second, 0)]
        halos = [neighbours(part, slabs) for part in middles]
        partials = [
            whole_again(None, base, at, [green_diag], [part], at, step, (size, 2, width, width))
            for part, (at, size) in zip(middles, second)
        ]
        result = None
        for partial, halo, (at, _) in zip(partials, halos, second):
            result = whole_again(result, partial, 0, [green_lower, green_upper], halo, at, step, green_lower.shape)
        return result

    return lax.cond(fits, packed_rest, whole_rest, parts, weights, *arrived)


def solution(mesh):
    return jax.shard_map(
        local,
        mesh=mesh,
        in_specs=(
            P("slab", "energy", None, None, None),
            P("slab", "energy", None, None, None),
            P("slab", "energy", None, None, None),
            P("slab", "energy", None, None, None),
            P("slab", None, None, "energy", None),
            P("slab", None),
        ),
        out_specs=P("slab", "energy", None, None, None),
        check_vma=False,
    )
```

```python
import functools

import jax
import jax.numpy as jnp
import numpy as np
from jax import lax
from jax.experimental import pallas as pl
from jax.experimental.pallas import tpu as pltpu
from jax.sharding import PartitionSpec as P

F32 = jnp.float32
BF16 = jnp.bfloat16
MIB = 1024 * 1024


def params(mebibytes=16):
    return pltpu.CompilerParams(vmem_limit_bytes=mebibytes * MIB)


def split(value):
    high = value.astype(BF16)
    return high, (value - high.astype(F32)).astype(BF16)


def dot(first, second, transposed=False):
    dims = (((1,), (1,)), ((), ())) if transposed else (((1,), (0,)), ((), ()))
    return lax.dot_general(first, second, dims, preferred_element_type=F32)


def stack(*parts):
    return jnp.concatenate(parts, axis=0)


def beside(*parts):
    return jnp.concatenate(parts, axis=1)


def dot_stacked(first, second):
    rows = first.shape[0] // 2
    both = dot(first, second[0])
    return both[:rows] + (both[rows:] + dot(first[:rows], second[1]))


def sandwich(green, middle):
    rows = green.shape[0] // 2
    first = dot_stacked(green, middle)
    out = dot(stack(*split(first), *split(turn_halves(first))), green, transposed=True)
    real, real_low, imag, imag_low = (out[i * rows : (i + 1) * rows] for i in range(4))
    return beside(real[:, :rows] + (real[:, rows:] + real_low[:, :rows]), imag[:, :rows] + (imag[:, rows:] + imag_low[:, :rows]))


def turn_halves(value):
    width = value.shape[1] // 2
    return beside(value[:, width:], -value[:, :width])


def packed_sandwich(green, middle, turned, spread):
    rows, inner = green.shape[0] // 2, middle[0].shape[0]
    out = dot(stack(*middle, *turned), green, transposed=True)
    real, real_low, imag, imag_low = (out[i * inner : (i + 1) * inner] for i in range(4))
    inside = beside(real[:, :rows] + (real[:, rows:] + real_low[:, :rows]), imag[:, :rows] + (imag[:, rows:] + imag_low[:, :rows]))
    high, low = (spread(part, beside(-part[:, rows:], part[:, :rows])) for part in split(inside))
    both = dot(green, high)
    return both[:rows] + (both[rows:] + dot(green[:rows], low))


def lane_of(value):
    return lax.broadcasted_iota(jnp.int32, value.shape, 1)


def turn_packed(value, extra):
    width = value.shape[1] // 2
    wide, narrow = value[:, :width], value[:, width:]
    lane = lane_of(wide)
    sign = jnp.where(lane < width // 2, 1.0, -1.0)
    wide = pltpu.roll(wide, width // 2, axis=1) * sign
    narrow = jnp.where(lane % (2 * extra) < extra, pltpu.roll(narrow, width - extra, axis=1), -pltpu.roll(narrow, extra, axis=1))
    return beside(wide, narrow)


def load_matrix(ref, index):
    lead = (0,) * (len(ref.shape) - 4)
    return beside(ref[lead + (index, 0)], ref[lead + (index, 1)])


def load_flat(ref, index):
    width = ref.shape[1]
    at = 2 * index * width
    return beside(ref[at : at + width, :], ref[at + width : at + 2 * width, :])


def load_rows(ref, index):
    groups, _, double, _ = ref.shape
    rows = double // 2
    return beside(*[stack(*[ref[r, index, p * rows : (p + 1) * rows, :] for r in range(groups)]) for p in (0, 1)])


def store_matrix(ref, index, value):
    width = value.shape[1] // 2
    lead = (0,) * (len(ref.shape) - 4)
    ref[lead + (index, 0)] = value[:, :width]
    ref[lead + (index, 1)] = value[:, width:]


def store_by_rows(ref, index, value):
    groups, _, rows, _, width = ref.shape
    for r in range(groups):
        for p in (0, 1):
            ref[r, p, :, index, :] = value[r * rows : (r + 1) * rows, p * width : (p + 1) * width]


def whole_term(green, middle):
    pairs = [stack(part, beside(-part[:, part.shape[1] // 2 :], part[:, : part.shape[1] // 2])) for part in split(middle)]
    return sandwich(stack(*split(green)), pairs)


def packed_term(green, middle_ref, index, size, extra):
    half = green.shape[1] // 4
    share = half // extra
    middle = beside(middle_ref[index], middle_ref[size + index // share])

    def spread(part, turned):
        return stack(part[:half], turned[:half], *([part[half:], turned[half:]] * share))

    return packed_sandwich(green, split(middle), split(turn_packed(middle, extra)), spread)


def matrix_spec(step, offset, width, lead):
    shape = (1,) * lead + (step, 2, width, width)
    return pl.BlockSpec(shape, lambda i: (0,) * lead + (i + offset, 0, 0, 0))


def flat_spec(step, width):
    return pl.BlockSpec((2 * step * width, width), lambda i: (i, 0))


def rows_spec(step, groups, rows, width):
    return pl.BlockSpec((groups, step, 2 * rows, width), lambda i: (0, i, 0, 0))


def in_any():
    return pl.BlockSpec(memory_space=pl.ANY)


def cost(micros):
    return pl.CostEstimate(flops=int(micros * 0.3 * 1.15e9), bytes_accessed=int(micros * 0.3 * 3.69e6), transcendentals=0)


def own_terms_kernel(step, green, sigma, out):
    for index in range(step):
        store_matrix(out, index, whole_term(load_matrix(green, index), load_matrix(sigma, index)))


def own_terms(green, sigma, step):
    _, energies, _, width, _ = green.shape
    return pl.pallas_call(
        functools.partial(own_terms_kernel, step),
        grid=(energies // step,),
        in_specs=[matrix_spec(step, 0, width, 1)] * 2,
        out_specs=matrix_spec(step, 0, width, 0),
        out_shape=jax.ShapeDtypeStruct((energies, 2, width, width), F32),
        compiler_params=params(60),
        cost_estimate=cost(0.35 * energies),
        name="own_terms",
    )(green, sigma)


def side_terms_kernel(step, total, lower, upper, before, after, out, send):
    for index in range(step):
        value = load_matrix(total, index)
        value = value + whole_term(load_matrix(lower, index), load_flat(before, index))
        value = value + whole_term(load_matrix(upper, index), load_flat(after, index))
        store_matrix(out, index, value)
        store_by_rows(send, index, value)


def side_terms(total, lower, upper, before, after, begin, size, groups, step):
    width = total.shape[-1]
    rows = width // groups
    at = begin // step
    return pl.pallas_call(
        functools.partial(side_terms_kernel, step),
        grid=(size // step,),
        in_specs=[matrix_spec(step, at, width, 0)] + [matrix_spec(step, at, width, 1)] * 2 + [flat_spec(step, width)] * 2,
        out_specs=[
            matrix_spec(step, 0, width, 0),
            pl.BlockSpec((groups, 2, rows, step, width), lambda i: (0, 0, 0, i, 0)),
        ],
        out_shape=[
            jax.ShapeDtypeStruct((size, 2, width, width), F32),
            jax.ShapeDtypeStruct((groups, 2, rows, size, width), F32),
        ],
        compiler_params=params(60),
        cost_estimate=cost(0.75 * size),
        name="side_terms",
    )(total, lower, upper, before, after)


def whole_again_kernel(step, count, aliased, *refs):
    refs = refs[1:] if aliased else refs
    base, greens, middles, out = refs[0], refs[1 : 1 + count], refs[1 + count : 1 + 2 * count], refs[-1]
    for index in range(step):
        value = load_matrix(base, index)
        for green, middle in zip(greens, middles):
            value = value + whole_term(load_matrix(green, index), load_rows(middle, index))
        store_matrix(out, index, value)


def whole_again(result, base, base_begin, greens, middles, begin, step, shape):
    groups, size, double, width = middles[0].shape
    count = len(greens)
    at = begin // step
    aliased = result is not None
    return pl.pallas_call(
        functools.partial(whole_again_kernel, step, count, aliased),
        grid=(size // step,),
        in_specs=[in_any()] * aliased
        + [matrix_spec(step, base_begin // step, width, 0)]
        + [matrix_spec(step, at, width, 1)] * count
        + [rows_spec(step, groups, double // 2, width)] * count,
        out_specs=matrix_spec(step, at if len(shape) == 5 else 0, width, len(shape) - 4),
        out_shape=jax.ShapeDtypeStruct(shape, F32),
        input_output_aliases={0: 0} if aliased else {},
        compiler_params=params(),
        cost_estimate=cost(0.3 * count * size),
        name="whole_again",
    )(*([result] * aliased), base, *greens, *middles)


def packed_again_kernel(step, bases, count, size, extra, aliased, *refs):
    refs = refs[1:] if aliased else refs
    base_refs, refs = refs[: len(bases)], refs[len(bases) :]
    greens, middles, out = refs[:count], refs[count : 2 * count], refs[-1]
    here = pl.program_id(0)
    for index in range(step):
        value = load_matrix(base_refs[0], index)
        for (begin, _), ref in zip(bases[1:], base_refs[1:]):
            value = jnp.where(here >= begin, load_matrix(ref, index), value)
        for green, middle in zip(greens, middles):
            value = value + packed_term(green[index], middle, here * step + index, size, extra)
        store_matrix(out, index, value)


def packed_again(result, bases, greens, middles, begin, size, step, shape, extra):
    span, cap, width = middles[0].shape
    count = len(greens)
    at = begin // step
    aliased = result is not None
    places = chunks_of([base.shape[0] // step for base in bases])
    specs = [
        pl.BlockSpec((step, 2, width, width), lambda i, start=start, steps=steps: (jnp.clip(i - start, 0, steps - 1), 0, 0, 0))
        for start, steps in places
    ]
    return pl.pallas_call(
        functools.partial(packed_again_kernel, step, places, count, size, extra, aliased),
        grid=(size // step,),
        in_specs=[in_any()] * aliased
        + specs
        + [pl.BlockSpec((step, 2 * width, 2 * width), lambda i: (i + at, 0, 0))] * count
        + [pl.BlockSpec((span, cap, width), lambda i: (0, 0, 0))] * count,
        out_specs=matrix_spec(step, at if len(shape) == 5 else 0, width, len(shape) - 4),
        out_shape=jax.ShapeDtypeStruct(shape, F32),
        input_output_aliases={0: 0} if aliased else {},
        compiler_params=params(),
        cost_estimate=cost(0.3 * count * size),
        name="packed_again",
    )(*([result] * aliased), *bases, *greens, *middles)


def pack_green_kernel(step, extra, place, *refs):
    count = len(refs) // 2
    width = place.shape[1] // 2
    share = width // (2 * extra)
    for green, out, which in zip(refs[:count], refs[count:], range(count)):
        for index in range(step):
            both = dot(stack(*split(load_matrix(green, index))), place[which])
            lane = lane_of(both) - width
            other = (lane >= 0) & (lane // (2 * extra) != index % share)
            out[index] = jnp.where(other, 0.0, both).astype(BF16)


def pack_green(greens, places, step, extra):
    _, energies, _, width, _ = greens[0].shape
    count = len(greens)
    return pl.pallas_call(
        functools.partial(pack_green_kernel, step, extra),
        grid=(energies // step,),
        in_specs=[pl.BlockSpec(places.shape, lambda i: (0, 0, 0))] + [matrix_spec(step, 0, width, 1)] * count,
        out_specs=[pl.BlockSpec((step, 2 * width, 2 * width), lambda i: (i, 0, 0))] * count,
        out_shape=[jax.ShapeDtypeStruct((energies, 2 * width, 2 * width), BF16)] * count,
        compiler_params=params(60),
        cost_estimate=cost(0.13 * count * energies),
        name="pack_green",
    )(places, *greens)


def pack_rows_kernel(rows, chosen, part, out):
    groups, _, _ = part.shape
    for at in range(out.shape[0]):
        block = stack(*[part[r, at * rows : (at + 1) * rows, :] for r in range(groups)])
        high, low = split(block)
        out[at] = dot(chosen[...], high) + dot(chosen[...], low)


def pack_rows(chosen, part, rows):
    groups, height, width = part.shape
    cap = chosen.shape[0]
    whole = pl.BlockSpec(memory_space=pltpu.VMEM)
    return pl.pallas_call(
        functools.partial(pack_rows_kernel, rows),
        in_specs=[whole, whole],
        out_specs=whole,
        out_shape=jax.ShapeDtypeStruct((height // rows, cap, width), F32),
        compiler_params=params(),
        cost_estimate=cost(1.5),
        name="pack_rows",
    )(chosen, part)


def apply_table(table, value, size):
    both = dot(table, value[0])
    return both[:size] + (both[size:] + dot(table[:size], value[1]))


def convolve_kernel(first, second, rows, extra, forth, back, weight_ref, final_ref, *refs):
    arrived, outputs, scratch = refs[: len(first)], refs[len(first) : len(first) + len(second)], refs[len(first) + len(second) :]
    groups, _, here, _, width = arrived[0].shape
    half = weight_ref.shape[3]
    total = 2 * half
    double = 2 * rows
    local = total // groups
    share = width // (2 * extra) if extra else 0
    spans = [(size + size // share) * rows if extra else size * double for _, size in second]
    leaving = [ref.reshape(groups * span, width) for ref, span in zip(outputs, spans)]

    def load(row, p):
        return stack(*[arrived[c][j, p, row] for j in range(groups) for c in range(len(first))])

    def store_whole(row, real, imag):
        kept = final_ref[pl.ds(row, 1), :] * (1.0 / total)
        for p, value in enumerate((-imag * kept, real * kept)):
            for j in range(groups):
                for c, (begin, size) in enumerate(second):
                    at = j * local + begin
                    leaving[c][pl.ds(j * spans[c] + p * rows + row, size, stride=double), :] = value[at : at + size]

    def store_packed(row, real, imag, spare):
        value = beside(-imag, real) * (1.0 / total)
        both = dot(stack(*split(value)), final_ref[...])
        both = both[:total] + both[total:]
        spare[...] = both[:, width:]
        quarter = [spare[pl.ds(q, total // share, stride=share), :] for q in range(share)]
        lane = lane_of(quarter[0]) // (2 * extra)
        narrow = quarter[0]
        for q in range(1, share):
            narrow = jnp.where(lane == q, quarter[q], narrow)
        for j in range(groups):
            for c, (begin, size) in enumerate(second):
                at = j * local + begin
                leaving[c][pl.ds(j * spans[c] + row, size, stride=rows), :] = both[at : at + size, :width]
                leaving[c][pl.ds(j * spans[c] + size * rows + row, size // share, stride=rows), :] = narrow[
                    at // share : (at + size) // share
                ]

    for pair in range(here // 2):
        at = (2 * pair, 2 * pair + 1)
        values = [[load(row, p) for row in at] for p in (0, 1)]
        backs = []
        for odd in (0, 1):
            sign = 1.0 - 2.0 * odd
            folded = [beside(*[value[:half] + sign * value[half:] for value in part]) for part in values]
            spectrum = apply_table(forth[odd], split(stack(*folded)), total)
            real, imag = spectrum[:half], spectrum[half:]
            weights = [beside(*[weight_ref[row, p, odd] for row in at]) for p in (0, 1)]
            weighed = split(stack(real * weights[0] - imag * weights[1], real * weights[1] + imag * weights[0]))
            backs.append(apply_table(back[odd], weighed, total))
        early, late = backs[0] + backs[1], backs[0] - backs[1]
        for index, row in enumerate(at):
            lanes = slice(index * width, (index + 1) * width)
            real = stack(early[:half, lanes], late[:half, lanes])
            imag = stack(early[half:, lanes], late[half:, lanes])
            place = pl.program_id(0) * here + row
            if extra:
                store_packed(place, real, imag, scratch[row])
            else:
                store_whole(place, real, imag)


def convolve(arrived, weights, final, first, second, extra):
    groups, _, rows, _, width = arrived[0].shape
    half = weights.shape[3]
    total = 2 * half
    here = min(rows, 4)
    if extra:
        share = width // (2 * extra)
        shapes = [(groups, (size + size // share) * rows, width) for _, size in second]
        scratch = [pltpu.VMEM((total, width), F32)] * here
    else:
        shapes = [(groups, size, 2 * rows, width) for _, size in second]
        scratch = []

    def fixed(shape):
        return pl.BlockSpec(shape, lambda i: (0,) * len(shape))

    return pl.pallas_call(
        functools.partial(convolve_kernel, first, second, rows, extra),
        grid=(rows // here,),
        in_specs=[fixed((2, 2 * total, total))] * 2
        + [pl.BlockSpec((here, 2, 2, half, width), lambda i: (i, 0, 0, 0, 0)), fixed(final.shape)]
        + [pl.BlockSpec((groups, 2, here, size, width), lambda i: (0, 0, i, 0, 0)) for _, size in first],
        out_specs=[fixed(shape) for shape in shapes],
        out_shape=[jax.ShapeDtypeStruct(shape, F32) for shape in shapes],
        scratch_shapes=scratch,
        compiler_params=params(60),
        cost_estimate=cost(0.2 * total / groups + 4.0),
        name="convolve",
    )(transform_tables(total, False), transform_tables(total, True), weights, final, *arrived)


def transform_tables(total, back):
    half = total // 2
    tables = []
    for odd in (0, 1):
        phase = (2 * np.arange(half)[:, None] + odd) * np.arange(half)[None, :] % total
        cosine, sine = np.cos(2.0 * np.pi / total * phase), np.sin(2.0 * np.pi / total * phase)
        table = np.block([[cosine, sine], [-sine, cosine]])
        tables.append((table.T if back else table).astype(np.float32))
    high = [table.astype(jnp.bfloat16) for table in tables]
    low = [(table - part.astype(np.float32)).astype(jnp.bfloat16) for table, part in zip(tables, high)]
    return jnp.asarray(np.stack([np.concatenate(parts, axis=0) for parts in zip(high, low)]))


def neighbours(value, count):
    up = [(i, i + 1) for i in range(count - 1)]
    down = [(i + 1, i) for i in range(count - 1)]
    return lax.ppermute(value, "slab", up), lax.ppermute(value, "slab", down)


def exchange(value):
    return lax.all_to_all(value, "energy", split_axis=0, concat_axis=0, tiled=True)


def tied(value, earlier):
    return lax.optimization_barrier((value, earlier))[0]


def chunks_of(sizes):
    return [(sum(sizes[:i]), size) for i, size in enumerate(sizes)]


def placement(pattern, rank, extra):
    width = pattern.shape[0]
    lane = jnp.arange(2 * width)
    narrow = lane - width
    imag = jnp.where(lane < width, lane // (width // 2), narrow % (2 * extra) // extra)
    slot = jnp.where(lane < width, lane % (width // 2), width // 2 + narrow % extra)
    source = jnp.arange(2 * width)
    hit = (source[:, None] // width == imag[None, :]) & (jnp.tile(rank, 2)[:, None] == slot[None, :])
    return (hit & (jnp.tile(pattern, 2)[:, None] > 0)).astype(BF16)


def local(green_diag, green_lower, green_upper, sigma_lesser, screened, pattern):
    groups = lax.axis_size("energy")
    slabs = lax.axis_size("slab")
    _, energies, _, width, _ = sigma_lesser.shape
    rows = width // groups
    total = screened.shape[1]
    step = 4
    extra = width // 8
    cap = width // 2 + extra
    first = chunks_of([energies // 4] * 4)
    second = chunks_of([energies // 2] * 2)

    mine = pattern[0].astype(F32)
    sent = [sigma_lesser[0, at : at + size].reshape(2 * size * width, width) for at, size in first]
    edge = sent[0].shape[0]
    sent[0] = stack(sent[0], jnp.broadcast_to(mine, (8, width)))
    own = own_terms(green_diag, sigma_lesser, 2 * step)
    weights = tied(screened[0], own).reshape(total // 2, 2, 2, rows, width).transpose(3, 2, 1, 0, 4)
    halos, bases, arrived = [neighbours(part, slabs) for part in sent[:2]], [], []
    patterns = jnp.stack([mine, halos[0][0][edge], halos[0][1][edge]])
    ranks = jnp.cumsum(patterns, axis=1).astype(jnp.int32) - 1
    places = jnp.stack([placement(patterns[side], ranks[side], extra) for side in range(3)])
    packed_greens = pack_green([green_diag, green_lower, green_upper], places, step, extra)
    for index, (at, size) in enumerate(first):
        if index + 2 < len(first):
            halos.append(neighbours(tied(sent[index + 2], (halos[index], own)), slabs))
        halo = tied(halos[index], (arrived[max(index - 2, 0)], packed_greens) if index else weights)
        base, send = side_terms(own, green_lower, green_upper, *halo, at, size, groups, 2 * step)
        bases.append(base)
        arrived.append(exchange(send))

    fits = lax.pmax(tied(jnp.sum(mine), bases[-1]), "slab") <= cap
    chosen = ((ranks[0][None, :] == jnp.arange(cap)[:, None]) & (mine[None, :] > 0)).astype(BF16)
    own_rows = lax.dynamic_slice_in_dim(mine, lax.axis_index("energy") * rows, rows)
    mask = own_rows[:, None] * mine[None, :]
    parts = convolve(arrived, weights, places[0], first, second, extra)

    def within(begin, size):
        return [base for base, (at, _) in zip(bases, first) if begin <= at < begin + size]

    def packed_rest(parts, weights, *arrived):
        packed, halos, partials = [], [], []
        for index, (part, (at, size)) in enumerate(zip(parts, second)):
            part = exchange(tied(part, (packed[0], partials[: index - 1])) if index else part)
            packed.append(pack_rows(chosen, tied(part, partials) if index else part, rows))
            halos.append(neighbours(packed[-1], slabs))
            partials.append(
                packed_again(
                    None, within(at, size), packed_greens[:1], packed[-1:], at, size, 2 * step, (size, 2, width, width), extra
                )
            )
        result = None
        for partial, halo, (at, size) in zip(partials, halos, second):
            result = packed_again(result, [partial], packed_greens[1:], halo, at, size, 2 * step, green_lower.shape, extra)
        return result

    def whole_rest(parts, weights, *arrived):
        base = jnp.concatenate(bases, axis=0)
        middles = [exchange(part) for part in convolve(arrived, weights, mask, first, second, 0)]
        halos = [neighbours(part, slabs) for part in middles]
        partials = [
            whole_again(None, base, at, [green_diag], [part], at, step, (size, 2, width, width))
            for part, (at, size) in zip(middles, second)
        ]
        result = None
        for partial, halo, (at, _) in zip(partials, halos, second):
            result = whole_again(result, partial, 0, [green_lower, green_upper], halo, at, step, green_lower.shape)
        return result

    return lax.cond(fits, packed_rest, whole_rest, parts, weights, *arrived)


def solution(mesh):
    return jax.shard_map(
        local,
        mesh=mesh,
        in_specs=(
            P("slab", "energy", None, None, None),
            P("slab", "energy", None, None, None),
            P("slab", "energy", None, None, None),
            P("slab", "energy", None, None, None),
            P("slab", None, None, "energy", None),
            P("slab", None),
        ),
        out_specs=P("slab", "energy", None, None, None),
        check_vma=False,
    )
```
